512 devices in a mesh: gx: 8 (over y), gy: 8 (over z_lo, core), gz: 8 (over z_hi, x).
Axes of the slice: x: 4, y: 8, z: 8 (z_hi: 2, z_lo: 4; z = z_hi * 4 + z_lo), core: 2. Of those that a mesh axis runs over, the one named last changes fastest.
Arguments:
- tokens: bfloat16 [1024, 8192], P('gz', ('gx', 'gy')), may hold values from -6 to 6
- gate_weight: bfloat16 [8192, 14336], P(('gx', 'gz'), 'gy'), may hold values from -0.0625 to 0.0625
- up_weight: bfloat16 [8192, 14336], P(('gx', 'gz'), 'gy'), may hold values from -0.0625 to 0.0625
- down_weight: bfloat16 [8192, 14336], P(('gx', 'gz'), 'gy'), may hold values from -0.046875 to 0.046875
- grad_mixed: bfloat16 [1024, 8192], P('gz', ('gx', 'gy')), may hold values from -6 to 6
Outputs:
- mixed: bfloat16 [1024, 8192], P('gz', ('gx', 'gy'))
- tokens_grad: bfloat16 [1024, 8192], P('gz', ('gx', 'gy'))
The draws below stay inside these ranges and needn't reach their ends.
All inputs are finite; a program needn't handle non-finite values.
Results may differ from the reference program's by a relative error of at most 0.0049.
Values may be sent and summed in bfloat16 or wider, within the bound.
No kernel may reach another device: no remote copies, remote signals or barrier semaphores. Data moves between devices by JAX's collectives and lax.ppermute only.
A program may use at most 64 MiB of HBM per device.

```python
import jax
import jax.numpy as jnp
from jax import lax

D = 8192
FF = 14336
TOKENS = 1024


def levels(key, dims, shards, least, top_value):
    loudness, own = 1.0, jax.random.fold_in(key, 6)
    for dim, shards_of in shards:
        steps = jnp.exp(jax.random.uniform(jax.random.fold_in(own, dim), (shards_of,), jnp.float32, least / len(shards), top_value / len(shards)))
        loudness = loudness * jnp.repeat(steps, dims[dim] // shards_of).reshape([-1 if axis == dim else 1 for axis in range(len(dims))])
    return loudness


def gaussian(key, extent, scale, most, pieces=(), held_as=jnp.bfloat16):
    loudness = levels(key, extent, pieces, -0.22, 0.18) if pieces else 1.0
    array = jax.random.normal(key, extent, jnp.float32) * scale * loudness
    return jnp.minimum(jnp.maximum(array, -most), most).astype(held_as)


def setup_inputs(seed: int = 0) -> dict:
    arg_keys = jax.random.split(jax.random.key(seed), 6)
    tokens = gaussian(arg_keys[0], (TOKENS, D), 1.0, 6.0, ((0, 8), (1, 64)))
    gate_weight = gaussian(arg_keys[1], (D, FF), D ** -0.5, 0.0625, ((0, 64), (1, 8)))
    up_weight = gaussian(arg_keys[2], (D, FF), D ** -0.5, 0.0625, ((0, 64), (1, 8)))
    down_weight = gaussian(arg_keys[3], (D, FF), FF ** -0.5, 0.046875, ((0, 64), (1, 8)))
    grad_mixed = gaussian(arg_keys[4], (TOKENS, D), 1.0, 6.0, ((0, 8), (1, 64)))
    return dict(tokens=tokens, gate_weight=gate_weight, up_weight=up_weight, down_weight=down_weight, grad_mixed=grad_mixed)


def reference(tokens, gate_weight, up_weight, down_weight, grad_mixed):
    gate_value = jnp.dot(tokens, gate_weight, preferred_element_type=jnp.float32)
    up_value = jnp.dot(tokens, up_weight, preferred_element_type=jnp.float32)
    silu_gate = jax.nn.silu(gate_value)
    hidden = (silu_gate * up_value).astype(jnp.bfloat16)
    contract = (((1,), (1,)), ((), ()))
    mixed = lax.dot_general(hidden, down_weight, contract, preferred_element_type=jnp.float32).astype(jnp.bfloat16)
    hidden_grad = jnp.dot(grad_mixed, down_weight, preferred_element_type=jnp.float32)
    sigmoid_gate = jax.nn.sigmoid(gate_value)
    gate_grad = (hidden_grad * up_value * sigmoid_gate * (1.0 + gate_value * (1.0 - sigmoid_gate))).astype(jnp.bfloat16)
    up_grad = (hidden_grad * silu_gate).astype(jnp.bfloat16)
    grad_terms = lax.dot_general(gate_grad, gate_weight, contract, preferred_element_type=jnp.float32)
    grad_terms = grad_terms + lax.dot_general(up_grad, up_weight, contract, preferred_element_type=jnp.float32)
    tokens_grad = grad_terms.astype(jnp.bfloat16)
    return (mixed, tokens_grad)
```

```python
import jax
import jax.numpy as jnp
from jax import lax
from jax.sharding import Mesh, PartitionSpec as P

AXES = ("y", "zl", "core", "zh", "x")
RING = ("zh", "zl", "core")
NT = (((1,), (1,)), ((), ()))
F32, BF16 = jnp.float32, jnp.bfloat16


def shift(values, step):
    return lax.ppermute(values, "x", [(i, (i + step) % 4) for i in range(4)])


def spread(values, axes, n):
    return lax.all_to_all(jnp.broadcast_to(values[None], (n, *values.shape)), axes, 0, 0, tiled=True)


def widen(values):
    blocks = spread(values, RING, 16).reshape(2, 2, 2, 2, 128, 128)
    return blocks.transpose(0, 4, 2, 3, 1, 5).reshape(256, 1024)


def swap(weight):
    return lax.all_to_all(weight, "zh", 1, 0, tiled=True)


def gather(block):
    half = block.shape[0] // 2
    left, right = shift(block, 1), shift(block, -1)
    far = jnp.concatenate([shift(left[:half], 1), shift(right[half:], -1)], axis=0)
    return jnp.concatenate([block, left, right, far], axis=0)


def to_relative(values, x):
    blocks = values.reshape(256, 4, 256)
    return jnp.concatenate(
        [lax.dynamic_index_in_dim(blocks, (x + k) % 4, 1, keepdims=False) for k in (0, 3, 1, 2)], axis=1
    )


def to_absolute(values, x):
    blocks = values.reshape(256, 4, 256)
    slots = jnp.array([0, 2, 3, 1])
    return jnp.stack(
        [lax.dynamic_index_in_dim(blocks, slots[(k - x) % 4], 1, keepdims=False) for k in range(4)], axis=1
    )


def combine(partial_value):
    parts = lax.all_to_all(partial_value.astype(BF16).reshape(8, 32, -1), "y", 0, 0, tiled=True)
    return jnp.sum(parts.astype(F32), axis=0)


def tokens_of(values):
    return spread(values, "y", 8).reshape(256, -1)


def narrow(values, x):
    terms = to_absolute(values, x).astype(BF16).reshape(2, 128, 2, 2, 2, 128)
    terms = terms.transpose(0, 4, 2, 3, 1, 5).reshape(16, 128, 128)
    parts = lax.all_to_all(terms, RING, 0, 0, tiled=True)
    return jnp.sum(parts.astype(F32), axis=0).astype(BF16)


def on_device(tokens, gate_weight, up_weight, down_weight, grad_mixed):
    x = lax.axis_index("x")
    gate = gather(swap(gate_weight))
    wide = to_relative(widen(tokens), x)
    gate_value = combine(jnp.dot(wide, gate, preferred_element_type=F32))
    up = gather(swap(up_weight))
    up_value = combine(jnp.dot(wide, up, preferred_element_type=F32))
    down = gather(swap(down_weight))
    wide_grad = to_relative(widen(grad_mixed), x)
    hidden_grad = combine(jnp.dot(wide_grad, down, preferred_element_type=F32))
    sig = jax.nn.sigmoid(gate_value)
    silu = gate_value * sig
    hidden = tokens_of((silu * up_value).astype(BF16))
    mixed = narrow(lax.dot_general(hidden, down, NT, preferred_element_type=F32), x)
    gate_grad = (hidden_grad * up_value * sig * (1.0 + gate_value * (1.0 - sig))).astype(BF16)
    up_grad = (hidden_grad * silu).astype(BF16)
    grads = tokens_of(jnp.concatenate([gate_grad, up_grad], axis=1))
    terms = lax.dot_general(grads[:, :896], gate, NT, preferred_element_type=F32)
    terms = terms + lax.dot_general(grads[:, 896:], up, NT, preferred_element_type=F32)
    return mixed, narrow(terms, x)


def solution(mesh):
    fine = Mesh(mesh.devices.reshape(8, 4, 2, 2, 4), AXES)
    acts = P(("zh", "x"), ("y", "zl", "core"))
    weights = P(("y", "zh", "x"), ("zl", "core"))
    return jax.shard_map(
        on_device,
        mesh=fine,
        in_specs=(acts, weights, weights, weights, acts),
        out_specs=(acts, acts),
        check_vma=False,
    )
```

```python
import jax
import jax.numpy as jnp
from jax import lax
from jax.experimental import pallas as pl
from jax.experimental.pallas import tpu as pltpu
from jax.sharding import Mesh, PartitionSpec as P

AXES = ("y", "zl", "core", "zh", "x")
RING = ("zh", "zl", "core")
NT = (((1,), (1,)), ((), ()))
F32, BF16 = jnp.float32, jnp.bfloat16
STEPS = (0, 3, 1, 2)


def shift(values, step):
    return lax.ppermute(values, "x", [(i, (i + step) % 4) for i in range(4)])


def swap(weight, zh):
    low, high = weight[:, :896], weight[:, 896:]
    other = lax.ppermute(jnp.where(zh == 0, high, low), "zh", [(0, 1), (1, 0)])
    return jnp.concatenate([jnp.where(zh == 0, low, high), other], axis=0)


def gather(block, by_left):
    left, right = shift(block, 1), shift(block, -1)
    far = shift(left, 1) if by_left else shift(right, -1)
    return block, left, right, far


def feature_block(place, slot, row):
    return ((place[1] + row) % 2) * 4 + (place[0] + STEPS[slot]) % 4


def partial_kernel(which, place, acts, b0, b1, b2, b3, out):
    total = None
    for slot, block in enumerate((b0, b1, b2, b3)):
        f0, f1 = feature_block(place, slot, 0), feature_block(place, slot, 1)
        wide = jnp.concatenate(
            [jnp.concatenate([acts[8 * t + f0, 0], acts[8 * t + f1, 0]], axis=1) for t in (0, 1)], axis=0
        )
        term = jnp.dot(wide, block[...], preferred_element_type=F32)
        total = term if total is None else total + term
    out[...] = total.astype(BF16)


def partial_value(which, place, acts, blocks):
    whole = pl.BlockSpec((256, 896), lambda i: (0, 0))
    return pl.pallas_call(
        lambda *refs: partial_kernel(which, *refs),
        grid=(1,),
        out_shape=jax.ShapeDtypeStruct((256, 896), BF16),
        in_specs=[
            pl.BlockSpec(memory_space=pltpu.SMEM),
            pl.BlockSpec((16, 1, 128, 128), lambda i: (0, which, 0, 0)),
            whole, whole, whole, whole,
        ],
        out_specs=whole,
        cost_estimate=pl.CostEstimate(flops=2 * 256 * 1024 * 896, bytes_accessed=3000000, transcendentals=0),
        compiler_params=pltpu.CompilerParams(vmem_limit_bytes=16 << 20),
    )(place, acts, *blocks)


def output_kernel(place, acts, *refs):
    gate, up, down, out = refs[:4], refs[4:8], refs[8:12], refs[12]
    hidden, gate_grad, up_grad = (acts[:, k].reshape(256, 896) for k in range(3))
    for slot in range(4):
        mixed = lax.dot_general(hidden, down[slot][...], NT, preferred_element_type=F32)
        grad = lax.dot_general(gate_grad, gate[slot][...], NT, preferred_element_type=F32)
        grad = grad + lax.dot_general(up_grad, up[slot][...], NT, preferred_element_type=F32)
        for row in (0, 1):
            f = feature_block(place, slot, row)
            for t in (0, 1):
                part = (slice(128 * t, 128 * t + 128), slice(128 * row, 128 * row + 128))
                out[8 * t + f, 0] = mixed[part].astype(BF16)
                out[8 * t + f, 1] = grad[part].astype(BF16)


def output_terms(place, acts, blocks):
    whole = pl.BlockSpec((256, 896), lambda i: (0, 0))
    return pl.pallas_call(
        output_kernel,
        grid=(1,),
        out_shape=jax.ShapeDtypeStruct((16, 2, 128, 128), BF16),
        in_specs=[pl.BlockSpec(memory_space=pltpu.SMEM), pl.BlockSpec((8, 3, 32, 896), lambda i: (0, 0, 0, 0))] + [whole] * 12,
        out_specs=pl.BlockSpec((16, 2, 128, 128), lambda i: (0, 0, 0, 0)),
        cost_estimate=pl.CostEstimate(flops=6 * 256 * 1024 * 896, bytes_accessed=8000000, transcendentals=0),
        compiler_params=pltpu.CompilerParams(vmem_limit_bytes=32 << 20),
    )(place, acts, *blocks)


def combine(partial):
    parts = lax.all_to_all(partial.reshape(8, 32, 896), "y", 0, 0, tiled=True)
    return jnp.sum(parts.astype(F32), axis=0)


def on_device(tokens, gate_weight, up_weight, down_weight, grad_mixed):
    x, zh = lax.axis_index("x"), lax.axis_index("zh")
    place = jnp.stack([x, zh])
    acts = lax.all_gather(jnp.stack([tokens, grad_mixed]), RING, axis=0)
    gate = gather(swap(gate_weight, zh), True)
    gate_value = combine(partial_value(0, place, acts, gate))
    up = gather(swap(up_weight, zh), False)
    up_value = combine(partial_value(0, place, acts, up))
    down = gather(swap(down_weight, zh), True)
    hidden_grad = combine(partial_value(1, place, acts, down))
    sig = jax.nn.sigmoid(gate_value)
    silu = gate_value * sig
    hidden = (silu * up_value).astype(BF16)
    gate_grad = (hidden_grad * up_value * sig * (1.0 + gate_value * (1.0 - sig))).astype(BF16)
    up_grad = (hidden_grad * silu).astype(BF16)
    rows = jnp.stack([hidden, gate_grad, up_grad])
    rows = lax.all_to_all(jnp.broadcast_to(rows[None], (8, 3, 32, 896)), "y", 0, 0, tiled=True)
    terms = lax.all_to_all(output_terms(place, rows, (*gate, *up, *down)), RING, 0, 0, tiled=True)
    both = jnp.sum(terms.astype(F32), axis=0).astype(BF16)
    return both[0], both[1]


def solution(mesh):
    fine = Mesh(mesh.devices.reshape(8, 4, 2, 2, 4), AXES)
    acts = P(("zh", "x"), ("y", "zl", "core"))
    weights = P(("y", "zh", "x"), ("zl", "core"))
    return jax.shard_map(
        on_device,
        mesh=fine,
        in_specs=(acts, weights, weights, weights, acts),
        out_specs=(acts, acts),
        check_vma=False,
    )
```

```python
import jax
import jax.numpy as jnp
from jax import lax
from jax.experimental import pallas as pl
from jax.experimental.pallas import tpu as pltpu
from jax.sharding import Mesh, PartitionSpec as P

AXES = ("y", "zl", "core", "zh", "x")
RING = ("zh", "zl", "core")
NT = (((1,), (1,)), ((), ()))
F32, BF16 = jnp.float32, jnp.bfloat16
STEPS = (0, 3, 1, 2)
GATE, DOWN, UP = 0, 1, 2
SMEM = pl.BlockSpec(memory_space=pltpu.SMEM)


def whole(*shape):
    return pl.BlockSpec(shape, lambda i: (0,) * len(shape))


def call(kernel, out_shapes, in_specs, flops, moved):
    return pl.pallas_call(
        kernel,
        grid=(1,),
        out_shape=[jax.ShapeDtypeStruct(s, BF16) for s in out_shapes],
        in_specs=[SMEM, *in_specs],
        out_specs=[whole(*s) for s in out_shapes],
        cost_estimate=pl.CostEstimate(flops=flops, bytes_accessed=moved, transcendentals=0),
        compiler_params=pltpu.CompilerParams(vmem_limit_bytes=32 << 20),
    )


def shift(values, step):
    return lax.ppermute(values, "x", [(i, (i + step) % 4) for i in range(4)])


def exchange(values, axis):
    return lax.ppermute(values, axis, [(0, 1), (1, 0)])


def split_kernel(place, gate, down, up, keep, send_gate, send_two):
    low = place[1] == 0
    for k, weight in enumerate((gate, down, up)):
        left, right = weight[:, :896], weight[:, 896:]
        keep[k] = jnp.where(low, left, right)
        away = jnp.where(low, right, left)
        if k == GATE:
            send_gate[0] = away
        else:
            send_two[k - 1] = away


def feature(place, own, x):
    return ((place[1] + (0 if own else 1)) % 2) * 4 + x


def act_tile(place, near, other, which, t, f):
    k = 4 * t + f // 2
    return jnp.where(f % 2 == place[2], near[k, which], other[k, which])


def fill(place, near, other, which, wide):
    for t in (0, 1):
        for slot in range(4):
            rows = pl.ds(128 * t, 128)
            wide[rows, pl.ds(128 * slot, 128)] = act_tile(place, near, other, which, t, feature(place, True, slot))
            x = (place[0] + STEPS[slot]) % 4
            wide[rows, pl.ds(512 + 128 * slot, 128)] = act_tile(place, near, other, which, t, feature(place, False, x))


def contract(wide, kept, moved):
    total = jnp.dot(wide[:, :512], kept.reshape(512, 896), preferred_element_type=F32)
    first, second = jnp.concatenate(moved[:2], axis=0), jnp.concatenate(moved[2:], axis=0)
    total = total + jnp.dot(wide[:, 512:768], first, preferred_element_type=F32)
    return total + jnp.dot(wide[:, 768:], second, preferred_element_type=F32)


def gate_kernel(place, near, other, kept, m0, m1, m2, m3, out, wide):
    fill(place, near, other, 0, wide)
    total = contract(wide, kept[:, 0], [m[0] for m in (m0, m1, m2, m3)])
    out[...] = total.astype(BF16).reshape(8, 32, 896)


def two_kernel(place, near, other, kept, m0, m1, m2, far_down, far_up, out, wide):
    for k, (which, far) in enumerate(((1, far_down), (0, far_up))):
        fill(place, near, other, which, wide)
        total = contract(wide, kept[:, k + 1], [m0[k], m1[k], m2[k], far[0]])
        out[:, k] = total.astype(BF16).reshape(8, 32, 896)


def partial_sums(kernel, n, place, operands):
    shape = (8, 32, 896) if n == 1 else (8, 2, 32, 896)
    return pl.pallas_call(
        kernel,
        grid=(1,),
        out_shape=jax.ShapeDtypeStruct(shape, BF16),
        in_specs=[SMEM] + [whole(*v.shape) for v in operands],
        out_specs=whole(*shape),
        scratch_shapes=[pltpu.VMEM((256, 1024), BF16)],
        cost_estimate=pl.CostEstimate(flops=n * 2 * 256 * 1024 * 896, bytes_accessed=n * 3000000, transcendentals=0),
        compiler_params=pltpu.CompilerParams(vmem_limit_bytes=32 << 20),
    )(place, *operands)


def output_kernel(place, acts, kept, g0, g1, g2, g3, m0, m1, m2, far_down, far_up, out):
    hidden, gate_grad, up_grad = (acts[:, k].reshape(256, 896) for k in range(3))

    def store(mixed, grad, slot, f):
        cols = slice(128 * slot, 128 * slot + 128)
        for t in (0, 1):
            rows = slice(128 * t, 128 * t + 128)
            out[8 * t + f, 0] = mixed[rows, cols].astype(BF16)
            out[8 * t + f, 1] = grad[rows, cols].astype(BF16)

    def terms(gate, down, up):
        mixed = lax.dot_general(hidden, down, NT, preferred_element_type=F32)
        grad = lax.dot_general(gate_grad, gate, NT, preferred_element_type=F32)
        return mixed, grad + lax.dot_general(up_grad, up, NT, preferred_element_type=F32)

    for pair in (0, 1):
        blocks = [kept[2 * pair : 2 * pair + 2, k].reshape(256, 896) for k in (GATE, DOWN, UP)]
        mixed, grad = terms(*blocks)
        for slot in (0, 1):
            store(mixed, grad, slot, feature(place, True, 2 * pair + slot))
    gates = [g[0] for g in (g0, g1, g2, g3)]
    downs = [m0[0], m1[0], m2[0], far_down[0]]
    ups = [m0[1], m1[1], m2[1], far_up[0]]
    for pair in (0, 1):
        blocks = [jnp.concatenate(v[2 * pair : 2 * pair + 2], axis=0) for v in (gates, downs, ups)]
        mixed, grad = terms(*blocks)
        for slot in (0, 1):
            x = (place[0] + STEPS[2 * pair + slot]) % 4
            store(mixed, grad, slot, feature(place, False, x))


def on_device(tokens, gate_weight, up_weight, down_weight, grad_mixed):
    place = jnp.stack([lax.axis_index("x"), lax.axis_index("zh"), lax.axis_index("core")])
    keep, send_gate, send_two = call(
        split_kernel, [(3, 128, 896), (1, 128, 896), (2, 128, 896)], [whole(128, 1792)] * 3, 0, 3000000
    )(place, gate_weight, down_weight, up_weight)
    kept = lax.all_gather(keep, "x", axis=0)
    gate = exchange(send_gate, "zh")
    two = exchange(send_two, "zh")

    acts = jnp.broadcast_to(jnp.stack([tokens, grad_mixed])[None], (8, 2, 128, 128))
    near = lax.all_to_all(acts, ("zh", "zl"), 0, 0, tiled=True)
    other = exchange(near, "core")

    gate_left, gate_right = shift(gate, 1), shift(gate, -1)
    gates = (gate, gate_left, gate_right, shift(gate_left, 1))
    gate_parts = lax.all_to_all(partial_sums(gate_kernel, 1, place, (near, other, kept, *gates)), "y", 0, 0, tiled=True)

    two_left, two_right = shift(two, 1), shift(two, -1)
    twos = (two, two_left, two_right, shift(two_left[:1], 1), shift(two_right[1:], -1))
    two_parts = lax.all_to_all(partial_sums(two_kernel, 2, place, (near, other, kept, *twos)), "y", 0, 0, tiled=True)

    gate_value = jnp.sum(gate_parts.astype(F32), axis=0)
    hidden_grad, up_value = (jnp.sum(two_parts[:, k].astype(F32), axis=0) for k in (0, 1))
    sig = jax.nn.sigmoid(gate_value)
    silu = gate_value * sig
    hidden = (silu * up_value).astype(BF16)
    gate_grad = (hidden_grad * up_value * sig * (1.0 + gate_value * (1.0 - sig))).astype(BF16)
    up_grad = (hidden_grad * silu).astype(BF16)
    rows = jnp.stack([hidden, gate_grad, up_grad])
    rows = lax.all_to_all(jnp.broadcast_to(rows[None], (8, 3, 32, 896)), "y", 0, 0, tiled=True)
    operands = (rows, kept, *gates, *twos)
    (terms,) = call(
        output_kernel, [(16, 2, 128, 128)], [whole(*v.shape) for v in operands], 6 * 256 * 1024 * 896, 8000000
    )(place, *operands)
    terms = lax.all_to_all(terms, RING, 0, 0, tiled=True)
    both = jnp.sum(terms.astype(F32), axis=0).astype(BF16)
    return both[0], both[1]


def solution(mesh):
    fine = Mesh(mesh.devices.reshape(8, 4, 2, 2, 4), AXES)
    acts = P(("zh", "x"), ("y", "zl", "core"))
    weights = P(("y", "zh", "x"), ("zl", "core"))
    return jax.shard_map(
        on_device,
        mesh=fine,
        in_specs=(acts, weights, weights, weights, acts),
        out_specs=(acts, acts),
        check_vma=False,
    )
```

```python
import jax
import jax.numpy as jnp
from jax import lax
from jax.experimental import pallas as pl
from jax.experimental.pallas import tpu as pltpu
from jax.sharding import Mesh, PartitionSpec as P

AXES = ("y", "zl", "core", "zh", "x")
NT = (((1,), (1,)), ((), ()))
F32, BF16 = jnp.float32, jnp.bfloat16
STEPS = (0, 3, 1, 2)
GATE, DOWN, UP = 0, 1, 2
WHICH = {GATE: 0, DOWN: 1, UP: 0}
HBM = pl.BlockSpec(memory_space=pltpu.HBM)
SMEM = pl.BlockSpec(memory_space=pltpu.SMEM)
BLOCK = (128, 896)


def call(kernel, outs, operands, scratch, flops, moved):
    return pl.pallas_call(
        kernel,
        out_shape=outs,
        in_specs=[SMEM] + [HBM] * (len(operands) - 1),
        out_specs=[HBM] * len(outs),
        scratch_shapes=scratch,
        cost_estimate=pl.CostEstimate(flops=flops, bytes_accessed=moved, transcendentals=0),
        compiler_params=pltpu.CompilerParams(vmem_limit_bytes=40 << 20),
    )(*operands)


def start(copies):
    for copy in copies:
        copy.start()
    return copies


def wait(copies):
    for copy in copies:
        copy.wait()


def shift(values, step):
    return lax.ppermute(values, "x", [(i, (i + step) % 4) for i in range(4)])


def exchange(values, axis):
    return lax.ppermute(values, axis, [(0, 1), (1, 0)])


def split_kernel(place, gate, down, up, keep, send_gate, send_down, send_up, sems):
    zh = place[1]
    low, high = pl.ds(0, 896), pl.ds(896, 896)

    def copies(mine, away):
        made = []
        for k, (weight, send) in enumerate(((gate, send_gate), (down, send_down), (up, send_up))):
            made.append(pltpu.make_async_copy(weight.at[:, mine], keep.at[k], sems.at[2 * k]))
            made.append(pltpu.make_async_copy(weight.at[:, away], send, sems.at[2 * k + 1]))
        return made

    @pl.when(zh == 0)
    def _():
        wait(start(copies(low, high)))

    @pl.when(zh == 1)
    def _():
        wait(start(copies(high, low)))


def acts_kernel(place, tokens, grad, out, sems):
    wait(start(
        [pltpu.make_async_copy(v, out.at[i, k], sems.at[2 * i + k]) for i in range(8) for k, v in enumerate((tokens, grad))]
    ))


def feature(place, own, x):
    return ((place[1] + (0 if own else 1)) % 2) * 4 + x


def came_from(place, slot):
    return (place[0] + STEPS[slot]) % 4


def load_weights(k, kept, moved, kept_v, moved_v, sems):
    made = [pltpu.make_async_copy(kept.at[:, k], kept_v.at[k], sems.at[5 * k])]
    for slot in range(4):
        made.append(pltpu.make_async_copy(moved[4 * k + slot], moved_v.at[k, slot], sems.at[5 * k + 1 + slot]))
    return made


def sums_kernel(place, near, other, kept, *refs):
    moved, out = refs[:12], refs[12]
    acts_v, kept_v, moved_v, wide, out_v, sems = refs[13:]
    acts = start(
        [pltpu.make_async_copy(near, acts_v.at[0], sems.at[15]), pltpu.make_async_copy(other, acts_v.at[1], sems.at[16])]
    )
    loads = [start(load_weights(k, kept, moved, kept_v, moved_v, sems)) for k in range(3)]
    wait(acts)
    for which in (0, 1):
        for t in (0, 1):
            for own in (True, False):
                for slot in range(4):
                    f = feature(place, own, slot if own else came_from(place, slot))
                    tile = acts_v[(f + place[2]) % 2, 4 * t + f // 2, which]
                    wide[which, pl.ds(128 * t, 128), pl.ds((0 if own else 512) + 128 * slot, 128)] = tile
    stores = []
    for k in range(3):
        wait(loads[k])
        which = WHICH[k]
        total = jnp.dot(wide[which, :, :512], kept_v[k].reshape(512, 896), preferred_element_type=F32)
        total = total + jnp.dot(wide[which, :, 512:], moved_v[k].reshape(512, 896), preferred_element_type=F32)
        out_v[k] = total.astype(BF16).reshape(8, 32, 896)
        stores += start([pltpu.make_async_copy(out_v.at[k], out.at[:, k], sems.at[17 + k])])
    wait(stores)


def output_kernel(place, acts, kept, *refs):
    moved, (mine, theirs) = refs[:12], refs[12:14]
    acts_v, kept_v, moved_v, out_v, sems = refs[14:]
    acts_in = start([pltpu.make_async_copy(acts.at[:, k], acts_v.at[k], sems.at[15 + k]) for k in range(3)])
    loads = [start(load_weights(k, kept, moved, kept_v, moved_v, sems)) for k in range(3)]
    wait(acts_in)
    hidden, gate_grad, up_grad = (acts_v[k].reshape(256, 896) for k in range(3))

    def store(terms, which, own):
        for slot in range(4):
            f = feature(place, own, slot if own else came_from(place, slot))
            for t in (0, 1):
                tile = terms[128 * t : 128 * t + 128, 128 * slot : 128 * slot + 128]
                out_v[(f + place[2]) % 2, 4 * t + f // 2, which] = tile

    def product(rows, blocks):
        return lax.dot_general(rows, blocks.reshape(512, 896), NT, preferred_element_type=F32)

    wait(loads[DOWN])
    store(product(hidden, kept_v[DOWN]), 0, True)
    store(product(hidden, moved_v[DOWN]), 0, False)
    wait(loads[GATE])
    wait(loads[UP])
    for own, held in ((True, kept_v), (False, moved_v)):
        store(product(gate_grad, held[GATE]) + product(up_grad, held[UP]), 1, own)
    wait(start(
        [pltpu.make_async_copy(out_v.at[0], mine, sems.at[18]), pltpu.make_async_copy(out_v.at[1], theirs, sems.at[19])]
    ))


def on_device(tokens, gate_weight, up_weight, down_weight, grad_mixed):
    place = jnp.stack([lax.axis_index("x"), lax.axis_index("zh"), lax.axis_index("core")])
    block = jax.ShapeDtypeStruct(BLOCK, BF16)
    keep, *sends = call(
        split_kernel,
        [jax.ShapeDtypeStruct((3, *BLOCK), BF16), block, block, block],
        (place, gate_weight, down_weight, up_weight),
        [pltpu.SemaphoreType.DMA((6,))], 0, 3000000,
    )
    kept = lax.all_gather(keep, "x", axis=0)
    arrived = [exchange(send, "zh") for send in sends]

    (acts,) = call(
        acts_kernel, [jax.ShapeDtypeStruct((8, 2, 128, 128), BF16)], (place, tokens, grad_mixed),
        [pltpu.SemaphoreType.DMA((16,))], 40000000000, 1000000,
    )
    near = lax.all_to_all(acts, ("zh", "zl"), 0, 0, tiled=True)
    other = exchange(near, "core")

    moved = []
    for k, block in enumerate(arrived):
        left, right = shift(block, 1), shift(block, -1)
        moved += [block, left, right, shift(right, -1) if k == DOWN else shift(left, 1)]

    weights_v = [pltpu.VMEM((3, 4, *BLOCK), BF16), pltpu.VMEM((3, 4, *BLOCK), BF16)]
    (parts,) = call(
        sums_kernel, [jax.ShapeDtypeStruct((8, 3, 32, 896), BF16)], (place, near, other, kept, *moved),
        [pltpu.VMEM((2, 8, 2, 128, 128), BF16), *weights_v, pltpu.VMEM((2, 256, 1024), BF16),
         pltpu.VMEM((3, 8, 32, 896), BF16), pltpu.SemaphoreType.DMA((20,))],
        6 * 256 * 1024 * 896, 8000000,
    )
    parts = lax.all_to_all(parts, "y", 0, 0, tiled=True)
    gate_value, hidden_grad, up_value = (jnp.sum(parts[:, k].astype(F32), axis=0) for k in range(3))
    sig = jax.nn.sigmoid(gate_value)
    silu = gate_value * sig
    hidden = (silu * up_value).astype(BF16)
    gate_grad = (hidden_grad * up_value * sig * (1.0 + gate_value * (1.0 - sig))).astype(BF16)
    up_grad = (hidden_grad * silu).astype(BF16)
    rows = jnp.stack([hidden, gate_grad, up_grad])
    rows = lax.all_to_all(jnp.broadcast_to(rows[None], (8, 3, 32, 896)), "y", 0, 0, tiled=True)
    terms = jax.ShapeDtypeStruct((8, 2, 128, 128), F32)
    mine, theirs = call(
        output_kernel, [terms, terms], (place, rows, kept, *moved),
        [pltpu.VMEM((3, 8, 32, 896), BF16), *weights_v, pltpu.VMEM((2, 8, 2, 128, 128), F32),
         pltpu.SemaphoreType.DMA((20,))],
        6 * 256 * 1024 * 896, 8000000,
    )
    terms = (mine + exchange(theirs, "core")).astype(BF16)
    terms = lax.all_to_all(terms, ("zh", "zl"), 0, 0, tiled=True)
    both = jnp.sum(terms.astype(F32), axis=0).astype(BF16)
    return both[0], both[1]


def solution(mesh):
    fine = Mesh(mesh.devices.reshape(8, 4, 2, 2, 4), AXES)
    acts = P(("zh", "x"), ("y", "zl", "core"))
    weights = P(("y", "zh", "x"), ("zl", "core"))
    return jax.shard_map(
        on_device,
        mesh=fine,
        in_specs=(acts, weights, weights, weights, acts),
        out_specs=(acts, acts),
        check_vma=False,
    )
```

```python
import jax
import jax.numpy as jnp
from jax import lax
from jax.experimental import pallas as pl
from jax.experimental.pallas import tpu as pltpu
from jax.sharding import Mesh, PartitionSpec as P

AXES = ("yh", "yl", "zu", "zv", "core", "zh", "x")
SIZES = (4, 2, 2, 2, 2, 2, 4)
SUMS = ("yh", "zh")
NEAR = ("yl", "zu", "zv")
NT = (((1,), (1,)), ((), ()))
F32, BF16 = jnp.float32, jnp.bfloat16
STEPS = (0, 3, 1, 2)
GATE, DOWN, UP = 0, 1, 2
WHICH = (0, 1, 0)
SMEM = pl.BlockSpec(memory_space=pltpu.SMEM)
VMEM = pl.BlockSpec(memory_space=pltpu.VMEM)
BLOCK = (128, 896)


def call(kernel, outs, operands, scratch, flops, moved):
    return pl.pallas_call(
        kernel,
        out_shape=outs,
        in_specs=[SMEM] + [VMEM] * (len(operands) - 1),
        out_specs=[VMEM] * len(outs),
        scratch_shapes=scratch,
        cost_estimate=pl.CostEstimate(flops=flops, bytes_accessed=moved, transcendentals=0),
        compiler_params=pltpu.CompilerParams(vmem_limit_bytes=24 << 20),
    )(*operands)


def shift(values, step):
    return lax.ppermute(values, "x", [(i, (i + step) % 4) for i in range(4)])


def exchange(values, axis):
    return lax.ppermute(values, axis, [(0, 1), (1, 0)])


def turn(values):
    return lax.ppermute(values, ("zu", "zh"), [(0, 0), (1, 2), (2, 1), (3, 3)])


def split_kernel(place, gate, down, up, keep, send_gate, send_down, send_up):
    low = place[1] == 0
    for k, (weight, send) in enumerate(((gate, send_gate), (down, send_down), (up, send_up))):
        left, right = weight[:, :896], weight[:, 896:]
        keep[k] = jnp.where(low, left, right)
        send[...] = jnp.where(low, right, left)


def acts_kernel(place, acts, out):
    for i in range(8):
        out[i] = acts[...]


def row_block(place, own, slot):
    if own:
        return place[1], slot
    return 1 - place[1], (place[0] + STEPS[slot]) % 4


def sums_kernel(place, near, other, kept, *refs):
    moved, out, wide = refs[:12], refs[12], refs[13]
    for own in (True, False):
        for slot in range(4):
            yl, x = row_block(place, own, slot)
            same = x % 2 == place[2]
            for t in (0, 1):
                i = 4 * yl + 2 * t + x // 2
                for which in (0, 1):
                    tile = jnp.where(same, near[i, which], other[i, which])
                    wide[which, pl.ds(128 * t, 128), pl.ds((0 if own else 512) + 128 * slot, 128)] = tile
    for k in range(3):
        acts = WHICH[k]
        total = jnp.dot(wide[acts, :, :512], kept[:, k].reshape(512, 896), preferred_element_type=F32)
        for pair in (0, 1):
            rows = jnp.concatenate([moved[4 * k + 2 * pair][...], moved[4 * k + 2 * pair + 1][...]], axis=0)
            cols = pl.ds(512 + 256 * pair, 256)
            total = total + jnp.dot(wide[acts, :, cols], rows, preferred_element_type=F32)
        out[:, k] = total.astype(BF16).reshape(8, 32, 896)


def output_kernel(place, acts, kept, *refs):
    moved, mine, theirs, held = refs[:12], refs[12], refs[13], refs[14]
    hidden, gate_grad, up_grad = (acts[:, k].reshape(256, 896) for k in range(3))

    def product(rows, block):
        return lax.dot_general(rows, block, NT, preferred_element_type=F32)

    for own in (True, False):
        for pair in (0, 1):
            if own:
                blocks = [kept[2 * pair : 2 * pair + 2, k].reshape(256, 896) for k in range(3)]
            else:
                blocks = [
                    jnp.concatenate([moved[4 * k + 2 * pair][...], moved[4 * k + 2 * pair + 1][...]], axis=0)
                    for k in range(3)
                ]
            mixed = product(hidden, blocks[DOWN])
            grad = product(gate_grad, blocks[GATE]) + product(up_grad, blocks[UP])
            for slot in (0, 1):
                yl, x = row_block(place, own, 2 * pair + slot)
                side = (x + place[2]) % 2
                for t in (0, 1):
                    part = (slice(128 * t, 128 * t + 128), slice(128 * slot, 128 * slot + 128))
                    held[side, 4 * yl + 2 * t + x // 2, 0] = mixed[part]
                    held[side, 4 * yl + 2 * t + x // 2, 1] = grad[part]
    mine[...] = held[0]
    theirs[...] = held[1]


def on_device(tokens, gate_weight, up_weight, down_weight, grad_mixed):
    place = jnp.stack([lax.axis_index("x"), lax.axis_index("yl"), lax.axis_index("core")])
    block = jax.ShapeDtypeStruct(BLOCK, BF16)
    keep, *sends = call(
        split_kernel,
        [jax.ShapeDtypeStruct((3, *BLOCK), BF16), block, block, block],
        (place, gate_weight, down_weight, up_weight), [], 0, 3000000,
    )
    kept = lax.all_gather(keep, "x", axis=0)
    arrived = [exchange(send, "yl") for send in sends]

    acts = turn(jnp.stack([tokens, grad_mixed]))
    (acts,) = call(
        acts_kernel, [jax.ShapeDtypeStruct((8, 2, 128, 128), BF16)], (place, acts), [], 40000000000, 1000000
    )
    near = lax.all_to_all(acts, NEAR, 0, 0, tiled=True)
    other = exchange(near, "core")

    moved = []
    for k, block in enumerate(arrived):
        left, right = shift(block, 1), shift(block, -1)
        moved += [block, left, right, shift(right, -1) if k == DOWN else shift(left, 1)]

    (parts,) = call(
        sums_kernel, [jax.ShapeDtypeStruct((8, 3, 32, 896), BF16)], (place, near, other, kept, *moved),
        [pltpu.VMEM((2, 256, 1024), BF16)], 6 * 256 * 1024 * 896, 8000000,
    )
    parts = lax.all_to_all(parts, SUMS, 0, 0, tiled=True)
    gate_value, hidden_grad, up_value = (jnp.sum(parts[:, k].astype(F32), axis=0) for k in range(3))
    sig = jax.nn.sigmoid(gate_value)
    silu = gate_value * sig
    hidden = (silu * up_value).astype(BF16)
    gate_grad = (hidden_grad * up_value * sig * (1.0 + gate_value * (1.0 - sig))).astype(BF16)
    up_grad = (hidden_grad * silu).astype(BF16)
    rows = jnp.stack([hidden, gate_grad, up_grad])
    rows = lax.all_to_all(jnp.broadcast_to(rows[None], (8, 3, 32, 896)), SUMS, 0, 0, tiled=True)
    terms = jax.ShapeDtypeStruct((8, 2, 128, 128), F32)
    mine, theirs = call(
        output_kernel, [terms, terms], (place, rows, kept, *moved),
        [pltpu.VMEM((2, 8, 2, 128, 128), F32)], 6 * 256 * 1024 * 896, 8000000,
    )
    terms = (mine + exchange(theirs, "core")).astype(BF16)
    terms = lax.all_to_all(terms, NEAR, 0, 0, tiled=True)
    both = turn(jnp.sum(terms.astype(F32), axis=0).astype(BF16))
    return both[0], both[1]


def solution(mesh):
    fine = Mesh(mesh.devices.reshape(SIZES), AXES)
    acts = P(("zh", "x"), ("yh", "yl", "zu", "zv", "core"))
    weights = P(("yh", "yl", "zh", "x"), ("zu", "zv", "core"))
    return jax.shard_map(
        on_device,
        mesh=fine,
        in_specs=(acts, weights, weights, weights, acts),
        out_specs=(acts, acts),
        check_vma=False,
    )
```

```python
import jax
import jax.numpy as jnp
from jax import lax
from jax.experimental import pallas as pl
from jax.experimental.pallas import tpu as pltpu
from jax.sharding import Mesh, PartitionSpec as P

AXES = ("yh", "yl", "zl", "core", "zh", "x")
SIZES = (4, 2, 4, 2, 2, 4)
RING = ("yl", "zl", "zh")
NT = (((1,), (1,)), ((), ()))
F32, BF16 = jnp.float32, jnp.bfloat16
STEPS = (0, 3, 1, 2)
GATE, DOWN, UP = 0, 1, 2
WHICH = (0, 1, 0)
SMEM = pl.BlockSpec(memory_space=pltpu.SMEM)
VMEM = pl.BlockSpec(memory_space=pltpu.VMEM)


def call(kernel, outs, operands, scratch, flops, moved):
    return pl.pallas_call(
        kernel,
        out_shape=outs,
        in_specs=[SMEM] + [VMEM] * (len(operands) - 1),
        out_specs=[VMEM] * len(outs),
        scratch_shapes=scratch,
        cost_estimate=pl.CostEstimate(flops=flops, bytes_accessed=moved, transcendentals=0),
        compiler_params=pltpu.CompilerParams(vmem_limit_bytes=24 << 20),
    )(*operands)


def shift(values, step):
    return lax.ppermute(values, "x", [(i, (i + step) % 4) for i in range(4)])


def exchange(values):
    return lax.ppermute(values, "core", [(0, 1), (1, 0)])


def turn(values):
    return lax.ppermute(values, ("yl", "core"), [(0, 0), (1, 2), (2, 1), (3, 3)])


def turn_across(values):
    pairs = [(4 * a + 2 * b + z, 4 * b + 2 * a + 1 - z) for a in (0, 1) for b in (0, 1) for z in (0, 1)]
    return lax.ppermute(values, ("yl", "core", "zh"), pairs)


def split_kernel(place, gate, down, up, keep, send):
    low = place[1] == 0
    for k, weight in enumerate((gate, down, up)):
        left, right = weight[:, :896], weight[:, 896:]
        rows = pl.ds(128 * k, 128)
        keep[rows] = jnp.where(low, left, right)
        send[rows] = jnp.where(low, right, left)


def acts_kernel(place, acts, out):
    for i in range(16):
        out[i] = acts[...]


def tile_index(place, own, slot, half):
    x = slot if own else (place[0] + STEPS[slot]) % 4
    zh = place[1] if own else 1 - place[1]
    t = place[2] if half == 0 else 1 - place[2]
    return 8 * (x % 2) + 2 * (2 * zh + x // 2) + t


def moved_rows(k, slot, block, left, right, far_low, far_high):
    if slot < 3:
        return (block, left, right)[slot][128 * k : 128 * k + 128]
    if k == 1:
        return jnp.concatenate([far_low[128:], far_high[:64]], axis=0)
    return far_low[:128] if k == 0 else far_high[64:]


def sums_kernel(place, acts, kept, *refs):
    moved, mine, theirs, wide = refs[:5], refs[5], refs[6], refs[7]
    for own in (True, False):
        for slot in range(4):
            for half in (0, 1):
                for which in (0, 1):
                    cols = pl.ds((0 if own else 512) + 128 * slot, 128)
                    wide[which, pl.ds(128 * half, 128), cols] = acts[tile_index(place, own, slot, half), which]
    for k in range(3):
        tokens = WHICH[k]
        rows = kept[:, pl.ds(128 * k, 128)].reshape(512, 896)
        total = jnp.dot(wide[tokens, :, :512], rows, preferred_element_type=F32)
        for pair in (0, 1):
            rows = jnp.concatenate([moved_rows(k, 2 * pair + i, *moved) for i in (0, 1)], axis=0)
            total = total + jnp.dot(wide[tokens, :, pl.ds(512 + 256 * pair, 256)], rows, preferred_element_type=F32)
        mine[:, k] = total[:128].reshape(4, 32, 896)
        theirs[:, k] = total[128:].reshape(4, 32, 896)


def output_kernel(place, near, other, kept, *refs):
    moved, out = refs[:5], refs[5]
    hidden, gate_grad, up_grad = (
        jnp.concatenate([near[:, k].reshape(128, 896), other[:, k].reshape(128, 896)], axis=0) for k in range(3)
    )

    def product(rows, block):
        return lax.dot_general(rows, block, NT, preferred_element_type=F32)

    for own in (True, False):
        for pair in (0, 1):
            if own:
                blocks = [kept[2 * pair : 2 * pair + 2, pl.ds(128 * k, 128)].reshape(256, 896) for k in range(3)]
            else:
                blocks = [
                    jnp.concatenate([moved_rows(k, 2 * pair + i, *moved) for i in (0, 1)], axis=0) for k in range(3)
                ]
            mixed = product(hidden, blocks[DOWN])
            grad = product(gate_grad, blocks[GATE]) + product(up_grad, blocks[UP])
            for slot in (0, 1):
                for half in (0, 1):
                    part = (slice(128 * half, 128 * half + 128), slice(128 * slot, 128 * slot + 128))
                    i = tile_index(place, own, 2 * pair + slot, half)
                    out[i, 0] = mixed[part].astype(BF16)
                    out[i, 1] = grad[part].astype(BF16)


def on_device(tokens, gate_weight, up_weight, down_weight, grad_mixed):
    place = jnp.stack([lax.axis_index("x"), lax.axis_index("zh"), lax.axis_index("core")])
    half = jax.ShapeDtypeStruct((384, 896), BF16)
    keep, send = call(split_kernel, [half, half], (place, gate_weight, down_weight, up_weight), [], 0, 3000000)
    block = turn_across(send)
    kept = lax.all_gather(turn(keep), "x", axis=0)

    acts = turn(jnp.stack([tokens, grad_mixed]))
    (acts,) = call(
        acts_kernel, [jax.ShapeDtypeStruct((16, 2, 128, 128), BF16)], (place, acts), [], 20000000000, 1000000
    )
    acts, _ = lax.optimization_barrier((acts, block))
    acts = lax.all_to_all(acts, RING, 0, 0, tiled=True)

    left, right = shift(block, 1), shift(block, -1)
    moved = (block, left, right, shift(left[:192], 1), shift(right[192:], -1))

    sums = jax.ShapeDtypeStruct((4, 3, 32, 896), F32)
    mine, theirs = call(
        sums_kernel, [sums, sums], (place, acts, kept, *moved), [pltpu.VMEM((2, 256, 1024), BF16)],
        6 * 256 * 1024 * 896, 8000000,
    )
    parts = lax.all_to_all((mine + exchange(theirs)).astype(BF16), "yh", 0, 0, tiled=True)
    gate_value, hidden_grad, up_value = (jnp.sum(parts[:, k].astype(F32), axis=0) for k in range(3))
    sig = jax.nn.sigmoid(gate_value)
    silu = gate_value * sig
    hidden = (silu * up_value).astype(BF16)
    gate_grad = (hidden_grad * up_value * sig * (1.0 + gate_value * (1.0 - sig))).astype(BF16)
    up_grad = (hidden_grad * silu).astype(BF16)
    rows = jnp.stack([hidden, gate_grad, up_grad])
    rows = lax.all_to_all(jnp.broadcast_to(rows[None], (4, 3, 32, 896)), "yh", 0, 0, tiled=True)
    (terms,) = call(
        output_kernel, [jax.ShapeDtypeStruct((16, 2, 128, 128), BF16)], (place, rows, exchange(rows), kept, *moved),
        [], 6 * 256 * 1024 * 896, 8000000,
    )
    terms = lax.all_to_all(terms, RING, 0, 0, tiled=True)
    both = turn(jnp.sum(terms.astype(F32), axis=0).astype(BF16))
    return both[0], both[1]


def solution(mesh):
    fine = Mesh(mesh.devices.reshape(SIZES), AXES)
    acts = P(("zh", "x"), ("yh", "yl", "zl", "core"))
    weights = P(("yh", "yl", "zh", "x"), ("zl", "core"))
    return jax.shard_map(
        on_device,
        mesh=fine,
        in_specs=(acts, weights, weights, weights, acts),
        out_specs=(acts, acts),
        check_vma=False,
    )
```

```python
import jax
import jax.numpy as jnp
from jax import lax
from jax.experimental import pallas as pl
from jax.experimental.pallas import tpu as pltpu
from jax.sharding import Mesh, PartitionSpec as P

AXES = ("y", "zl", "core", "zh", "x")
SIZES = (8, 4, 2, 2, 4)
RING = ("zh", "zl")
NT = (((1,), (1,)), ((), ()))
F32, BF16 = jnp.float32, jnp.bfloat16
STEPS = (0, 3, 1, 2)
GATE, DOWN, UP = 0, 1, 2
WHICH = (0, 1, 0)
SMEM = pl.BlockSpec(memory_space=pltpu.SMEM)
VMEM = pl.BlockSpec(memory_space=pltpu.VMEM)


def call(kernel, outs, operands, scratch, flops, moved):
    return pl.pallas_call(
        kernel,
        out_shape=outs,
        in_specs=[SMEM] + [VMEM] * (len(operands) - 1),
        out_specs=[VMEM] * len(outs),
        scratch_shapes=scratch,
        cost_estimate=pl.CostEstimate(flops=flops, bytes_accessed=moved, transcendentals=0),
        compiler_params=pltpu.CompilerParams(vmem_limit_bytes=12 << 20),
    )(*operands)


def shift(values, step):
    return lax.ppermute(values, "x", [(i, (i + step) % 4) for i in range(4)])


def exchange(values, axis):
    return lax.ppermute(values, axis, [(0, 1), (1, 0)])


def split_kernel(place, gate, down, up, keep, send):
    low = place[1] == 0
    for k, weight in enumerate((gate, down, up)):
        left, right = weight[:, :896], weight[:, 896:]
        rows = pl.ds(128 * k, 128)
        keep[rows] = jnp.where(low, left, right)
        send[rows] = jnp.where(low, right, left)


def table_kernel(place, out):
    for other_zh in (0, 1):
        for slot in range(4):
            zh = 1 - place[1] if other_zh else place[1]
            out[4 * other_zh + slot] = 4 * zh + (place[0] + STEPS[slot]) % 4
    out[8] = place[2]


def own_kernel(place, keep, block, out):
    for k in range(3):
        out[0, k] = keep[128 * k : 128 * k + 128]
        out[1, k] = block[128 * k : 128 * k + 128]


def spread_kernel(place, tokens, grad, out):
    for i in range(8):
        out[i, 0] = tokens[...]
        out[i, 1] = grad[...]


def rows_of(k, other_zh, pair, own, kept, moved):
    came, rows = (moved if other_zh else kept), slice(128 * k, 128 * k + 128)
    if pair:
        return jnp.concatenate([came[1][rows], came[2][rows]], axis=0)
    return jnp.concatenate([own[other_zh, k], came[0][rows]], axis=0)


def sums_kernel(table, near, other, own, *refs):
    kept, moved, out, wide = refs[:3], refs[3:6], refs[6], refs[7]
    for other_zh in (0, 1):
        for slot in range(4):
            f = table[4 * other_zh + slot]
            same = f % 2 == table[8]
            for t in (0, 1):
                for which in (0, 1):
                    tile = jnp.where(same, near[4 * t + f // 2, which], other[4 * t + f // 2, which])
                    wide[which, pl.ds(128 * t, 128), pl.ds(512 * other_zh + 128 * slot, 128)] = tile
    for k in range(3):
        total = None
        for other_zh in (0, 1):
            for pair in (0, 1):
                rows = rows_of(k, other_zh, pair, own, kept, moved)
                cols = pl.ds(512 * other_zh + 256 * pair, 256)
                term = jnp.dot(wide[WHICH[k], :, cols], rows, preferred_element_type=F32)
                total = term if total is None else total + term
        out[:, k] = total.astype(BF16).reshape(8, 32, 896)


def output_kernel(table, acts, own, *refs):
    kept, moved, mine, theirs, held = refs[:3], refs[3:6], refs[6], refs[7], refs[8]
    hidden, gate_grad, up_grad = (acts[:, k].reshape(256, 896) for k in range(3))

    def product(rows, block):
        return lax.dot_general(rows, block, NT, preferred_element_type=F32)

    for other_zh in (0, 1):
        for pair in (0, 1):
            gate, down, up = (rows_of(k, other_zh, pair, own, kept, moved) for k in range(3))
            mixed = product(hidden, down)
            grad = product(gate_grad, gate) + product(up_grad, up)
            for slot in (0, 1):
                f = table[4 * other_zh + 2 * pair + slot]
                side = (f + table[8]) % 2
                for t in (0, 1):
                    part = (slice(128 * t, 128 * t + 128), slice(128 * slot, 128 * slot + 128))
                    held[side, 4 * t + f // 2, 0] = mixed[part]
                    held[side, 4 * t + f // 2, 1] = grad[part]
    mine[...] = held[0]
    theirs[...] = held[1]


def on_device(tokens, gate_weight, up_weight, down_weight, grad_mixed):
    place = jnp.stack([lax.axis_index("x"), lax.axis_index("zh"), lax.axis_index("core")])
    half = jax.ShapeDtypeStruct((384, 896), BF16)
    keep, send = call(split_kernel, [half, half], (place, gate_weight, down_weight, up_weight), [], 0, 3000000)
    block = exchange(send, "zh")
    kept = (shift(keep, 1), shift(keep, -1), shift(keep, 2))
    (own,) = call(
        own_kernel, [jax.ShapeDtypeStruct((2, 3, 128, 896), BF16)], (place, keep, block), [], 30000000000, 2800000
    )
    block, own, kept, tokens = lax.optimization_barrier((block, own, kept, tokens))
    weights = (own, *kept, shift(block, 1), shift(block, -1), shift(block, 2))
    (acts,) = call(
        spread_kernel, [jax.ShapeDtypeStruct((8, 2, 128, 128), BF16)], (place, tokens, grad_mixed), [], 30000000000, 1000000
    )
    table = pl.pallas_call(
        table_kernel,
        out_shape=jax.ShapeDtypeStruct((9,), jnp.int32),
        in_specs=[SMEM],
        out_specs=SMEM,
        cost_estimate=pl.CostEstimate(flops=30000000000, bytes_accessed=64, transcendentals=0),
    )(place)
    near, table = lax.optimization_barrier((lax.all_to_all(acts, RING, 0, 0, tiled=True), table))

    (parts,) = call(
        sums_kernel, [jax.ShapeDtypeStruct((8, 3, 32, 896), BF16)],
        (table, near, exchange(near, "core"), *weights), [pltpu.VMEM((2, 256, 1024), BF16)],
        6 * 256 * 1024 * 896, 8000000,
    )
    parts = lax.all_to_all(parts, "y", 0, 0, tiled=True)
    gate_value, hidden_grad, up_value = (jnp.sum(parts[:, k].astype(F32), axis=0) for k in range(3))
    sig = jax.nn.sigmoid(gate_value)
    silu = gate_value * sig
    hidden = (silu * up_value).astype(BF16)
    gate_grad = (hidden_grad * up_value * sig * (1.0 + gate_value * (1.0 - sig))).astype(BF16)
    up_grad = (hidden_grad * silu).astype(BF16)
    rows = jnp.stack([hidden, gate_grad, up_grad])
    rows = lax.all_to_all(jnp.broadcast_to(rows[None], (8, 3, 32, 896)), "y", 0, 0, tiled=True)
    terms = jax.ShapeDtypeStruct((8, 2, 128, 128), F32)
    mine, theirs = call(
        output_kernel, [terms, terms], (table, rows, *weights), [pltpu.VMEM((2, 8, 2, 128, 128), F32)],
        6 * 256 * 1024 * 896, 8000000,
    )
    terms = (mine + exchange(theirs, "core")).astype(BF16)
    terms = lax.all_to_all(terms, RING, 0, 0, tiled=True)
    both = jnp.sum(terms.astype(F32), axis=0).astype(BF16)
    return both[0], both[1]


def solution(mesh):
    fine = Mesh(mesh.devices.reshape(SIZES), AXES)
    acts = P(("zh", "x"), ("y", "zl", "core"))
    weights = P(("y", "zh", "x"), ("zl", "core"))
    return jax.shard_map(
        on_device,
        mesh=fine,
        in_specs=(acts, weights, weights, weights, acts),
        out_specs=(acts, acts),
        check_vma=False,
    )
```

```python
import jax
import jax.numpy as jnp
from jax import lax
from jax.experimental import pallas as pl
from jax.experimental.pallas import tpu as pltpu
from jax.sharding import Mesh, PartitionSpec as P

AXES = ("y", "zl", "core", "zh", "x")
SIZES = (8, 4, 2, 2, 4)
RING = ("zh", "zl")
NT = (((1,), (1,)), ((), ()))
F32, BF16 = jnp.float32, jnp.bfloat16
STEPS = (0, 3, 1, 2)
GATE, DOWN, UP = 0, 1, 2
WHICH = (0, 1, 0)
SMEM = pl.BlockSpec(memory_space=pltpu.SMEM)
VMEM = pl.BlockSpec(memory_space=pltpu.VMEM)


def call(kernel, outs, operands, scratch, flops, moved):
    return pl.pallas_call(
        kernel,
        out_shape=outs,
        in_specs=[SMEM] + [VMEM] * (len(operands) - 1),
        out_specs=[VMEM] * len(outs),
        scratch_shapes=scratch,
        cost_estimate=pl.CostEstimate(flops=flops, bytes_accessed=moved, transcendentals=0),
        compiler_params=pltpu.CompilerParams(vmem_limit_bytes=12 << 20),
    )(*operands)


def shift(values, step):
    return lax.ppermute(values, "x", [(i, (i + step) % 4) for i in range(4)])


def exchange(values, axis):
    return lax.ppermute(values, axis, [(0, 1), (1, 0)])


def split_kernel(place, gate, down, up, keep, send):
    low = place[1] == 0
    for k, weight in enumerate((gate, down, up)):
        left, right = weight[:, :896], weight[:, 896:]
        rows = pl.ds(128 * k, 128)
        keep[rows] = jnp.where(low, left, right)
        send[rows] = jnp.where(low, right, left)


def table_kernel(place, out):
    for other_zh in (0, 1):
        for slot in range(4):
            zh = 1 - place[1] if other_zh else place[1]
            out[4 * other_zh + slot] = 4 * zh + (place[0] + STEPS[slot]) % 4
    out[8] = place[2]


def pack_kernel(place, b0, b1, b2, b3, out):
    for slot, block in enumerate((b0, b1, b2, b3)):
        for k in range(3):
            out[k, 128 * slot : 128 * slot + 128] = block[128 * k : 128 * k + 128]


def hold_kernel(place, block, out):
    out[...] = block[...]


def spread_kernel(place, tokens, grad, out):
    for i in range(8):
        out[i, 0] = tokens[...]
        out[i, 1] = grad[...]


def sums_kernel(table, near, other, kept, moved, out, wide):
    for other_zh in (0, 1):
        for slot in range(4):
            f = table[4 * other_zh + slot]
            same = f % 2 == table[8]
            for t in (0, 1):
                for which in (0, 1):
                    tile = jnp.where(same, near[4 * t + f // 2, which], other[4 * t + f // 2, which])
                    wide[which, pl.ds(128 * t, 128), pl.ds(512 * other_zh + 128 * slot, 128)] = tile
    for k in range(3):
        total = jnp.dot(wide[WHICH[k], :, :512], kept[k], preferred_element_type=F32)
        total = total + jnp.dot(wide[WHICH[k], :, 512:], moved[k], preferred_element_type=F32)
        out[:, k] = total.astype(BF16).reshape(8, 32, 896)


def output_kernel(table, acts, kept, moved, mine, theirs, held):
    hidden, gate_grad, up_grad = (acts[:, k].reshape(256, 896) for k in range(3))

    def product(rows, block):
        return lax.dot_general(rows, block, NT, preferred_element_type=F32)

    for other_zh, rows in enumerate((kept, moved)):
        mixed = product(hidden, rows[DOWN])
        grad = product(gate_grad, rows[GATE]) + product(up_grad, rows[UP])
        for slot in range(4):
            f = table[4 * other_zh + slot]
            side = (f + table[8]) % 2
            for t in (0, 1):
                part = (slice(128 * t, 128 * t + 128), slice(128 * slot, 128 * slot + 128))
                held[side, 4 * t + f // 2, 0] = mixed[part]
                held[side, 4 * t + f // 2, 1] = grad[part]
    mine[...] = held[0]
    theirs[...] = held[1]


def on_device(tokens, gate_weight, up_weight, down_weight, grad_mixed):
    place = jnp.stack([lax.axis_index("x"), lax.axis_index("zh"), lax.axis_index("core")])
    half = jax.ShapeDtypeStruct((384, 896), BF16)
    keep, send = call(split_kernel, [half, half], (place, gate_weight, down_weight, up_weight), [], 0, 3000000)
    block = exchange(send, "zh")
    kept = (shift(keep, 1), shift(keep, -1), shift(keep, 2))
    packed = jax.ShapeDtypeStruct((3, 512, 896), BF16)
    (first,) = call(pack_kernel, [packed], (place, keep, *kept), [], 0, 0)
    (hold,) = call(hold_kernel, [half], (place, block), [], 30000000000, 1400000)
    block, first, tokens = lax.optimization_barrier((hold, first, tokens))
    moved = (block, shift(block, 1), shift(block, -1), shift(block, 2))
    (second,) = call(pack_kernel, [packed], (place, *moved), [], 0, 0)
    weights = (first, second)
    (acts,) = call(
        spread_kernel, [jax.ShapeDtypeStruct((8, 2, 128, 128), BF16)], (place, tokens, grad_mixed), [], 30000000000, 1000000
    )
    table = pl.pallas_call(
        table_kernel,
        out_shape=jax.ShapeDtypeStruct((9,), jnp.int32),
        in_specs=[SMEM],
        out_specs=SMEM,
        cost_estimate=pl.CostEstimate(flops=30000000000, bytes_accessed=64, transcendentals=0),
    )(place)
    near, table = lax.optimization_barrier((lax.all_to_all(acts, RING, 0, 0, tiled=True), table))

    (parts,) = call(
        sums_kernel, [jax.ShapeDtypeStruct((8, 3, 32, 896), BF16)],
        (table, near, exchange(near, "core"), *weights), [pltpu.VMEM((2, 256, 1024), BF16)],
        6 * 256 * 1024 * 896, 8000000,
    )
    parts = lax.all_to_all(parts, "y", 0, 0, tiled=True)
    gate_value, hidden_grad, up_value = (jnp.sum(parts[:, k].astype(F32), axis=0) for k in range(3))
    sig = jax.nn.sigmoid(gate_value)
    silu = gate_value * sig
    hidden = (silu * up_value).astype(BF16)
    gate_grad = (hidden_grad * up_value * sig * (1.0 + gate_value * (1.0 - sig))).astype(BF16)
    up_grad = (hidden_grad * silu).astype(BF16)
    rows = jnp.stack([hidden, gate_grad, up_grad])
    rows = lax.all_to_all(jnp.broadcast_to(rows[None], (8, 3, 32, 896)), "y", 0, 0, tiled=True)
    terms = jax.ShapeDtypeStruct((8, 2, 128, 128), F32)
    mine, theirs = call(
        output_kernel, [terms, terms], (table, rows, *weights), [pltpu.VMEM((2, 8, 2, 128, 128), F32)],
        6 * 256 * 1024 * 896, 8000000,
    )
    terms = (mine + exchange(theirs, "core")).astype(BF16)
    terms = lax.all_to_all(terms, RING, 0, 0, tiled=True)
    both = jnp.sum(terms.astype(F32), axis=0).astype(BF16)
    return both[0], both[1]


def solution(mesh):
    fine = Mesh(mesh.devices.reshape(SIZES), AXES)
    acts = P(("zh", "x"), ("y", "zl", "core"))
    weights = P(("y", "zh", "x"), ("zl", "core"))
    return jax.shard_map(
        on_device,
        mesh=fine,
        in_specs=(acts, weights, weights, weights, acts),
        out_specs=(acts, acts),
        check_vma=False,
    )
```

```python
import jax
import jax.numpy as jnp
from jax import lax
from jax.experimental import pallas as pl
from jax.experimental.pallas import tpu as pltpu
from jax.sharding import Mesh, PartitionSpec as P

AXES = ("y", "zl", "core", "zh", "x")
SIZES = (8, 4, 2, 2, 4)
RING = ("zh", "zl")
NT = (((1,), (1,)), ((), ()))
F32, BF16 = jnp.float32, jnp.bfloat16
STEPS = (0, 3, 1, 2)
GATE, DOWN, UP = 0, 1, 2
WHICH = (0, 1, 0)
SMEM = pl.BlockSpec(memory_space=pltpu.SMEM)
VMEM = pl.BlockSpec(memory_space=pltpu.VMEM)


def call(kernel, outs, operands, scratch, flops, moved):
    return pl.pallas_call(
        kernel,
        out_shape=outs,
        in_specs=[SMEM] + [VMEM] * (len(operands) - 1),
        out_specs=[VMEM] * len(outs),
        scratch_shapes=scratch,
        cost_estimate=pl.CostEstimate(flops=flops, bytes_accessed=moved, transcendentals=0),
        compiler_params=pltpu.CompilerParams(vmem_limit_bytes=12 << 20),
    )(*operands)


def shift(values, step):
    return lax.ppermute(values, "x", [(i, (i + step) % 4) for i in range(4)])


def exchange(values, axis):
    return lax.ppermute(values, axis, [(0, 1), (1, 0)])


def split_kernel(place, gate, down, up, keep, send):
    low = place[1] == 0
    for k, weight in enumerate((gate, down, up)):
        left, right = weight[:, :896], weight[:, 896:]
        rows = pl.ds(128 * k, 128)
        keep[rows] = jnp.where(low, left, right)
        send[rows] = jnp.where(low, right, left)


def table_kernel(place, out):
    for other_zh in (0, 1):
        for slot in range(4):
            zh = 1 - place[1] if other_zh else place[1]
            out[4 * other_zh + slot] = 4 * zh + (place[0] + STEPS[slot]) % 4
    out[8] = place[2]


def pack_kernel(place, b0, b1, b2, b3, out):
    for slot, block in enumerate((b0, b1, b2, b3)):
        for k in range(3):
            out[k, 128 * slot : 128 * slot + 128] = block[128 * k : 128 * k + 128]


def hold_kernel(place, block, out):
    out[...] = block[...]


def spread_kernel(place, tokens, grad, out):
    for i in range(8):
        out[i, 0] = tokens[...]
        out[i, 1] = grad[...]


def sums_kernel(table, near, other, kept, moved, out, wide):
    for other_zh in (0, 1):
        for slot in range(4):
            f = table[4 * other_zh + slot]
            same = f % 2 == table[8]
            for t in (0, 1):
                for which in (0, 1):
                    tile = jnp.where(same, near[4 * t + f // 2, which], other[4 * t + f // 2, which])
                    wide[which, pl.ds(128 * t, 128), pl.ds(512 * other_zh + 128 * slot, 128)] = tile
    for k in range(3):
        total = jnp.dot(wide[WHICH[k], :, :512], kept[k], preferred_element_type=F32)
        total = total + jnp.dot(wide[WHICH[k], :, 512:], moved[k], preferred_element_type=F32)
        out[:, k] = total.astype(BF16).reshape(8, 32, 896)


def output_kernel(table, acts, kept, moved, mine, theirs, held):
    hidden, gate_grad, up_grad = (acts[:, k].reshape(256, 896) for k in range(3))

    def product(rows, block):
        return lax.dot_general(rows, block, NT, preferred_element_type=F32)

    for other_zh, rows in enumerate((kept, moved)):
        mixed = product(hidden, rows[DOWN])
        grad = product(gate_grad, rows[GATE]) + product(up_grad, rows[UP])
        for slot in range(4):
            f = table[4 * other_zh + slot]
            side = (f + table[8]) % 2
            for t in (0, 1):
                part = (slice(128 * t, 128 * t + 128), slice(128 * slot, 128 * slot + 128))
                held[side, 4 * t + f // 2, 0] = mixed[part]
                held[side, 4 * t + f // 2, 1] = grad[part]
    mine[...] = held[0]
    theirs[...] = held[1]


def on_device(tokens, gate_weight, up_weight, down_weight, grad_mixed):
    place = jnp.stack([lax.axis_index("x"), lax.axis_index("zh"), lax.axis_index("core")])
    half = jax.ShapeDtypeStruct((384, 896), BF16)
    keep, send = call(split_kernel, [half, half], (place, gate_weight, down_weight, up_weight), [], 0, 3000000)
    block = exchange(send, "zh")
    kept = (shift(keep, 1), shift(keep, -1), shift(keep, 2))
    packed = jax.ShapeDtypeStruct((3, 512, 896), BF16)
    (hold,) = call(hold_kernel, [half], (place, block), [], 30000000000, 1400000)
    block, left = lax.optimization_barrier((hold, kept[0]))
    moved = (block, shift(block, 1), shift(block, -1), shift(block, 2))
    (first,) = call(pack_kernel, [packed], (place, keep, left, *kept[1:]), [], 0, 0)
    first, tokens = lax.optimization_barrier((first, tokens))
    (second,) = call(pack_kernel, [packed], (place, *moved), [], 0, 0)
    weights = (first, second)
    (acts,) = call(
        spread_kernel, [jax.ShapeDtypeStruct((8, 2, 128, 128), BF16)], (place, tokens, grad_mixed), [], 0, 0
    )
    table = pl.pallas_call(
        table_kernel,
        out_shape=jax.ShapeDtypeStruct((9,), jnp.int32),
        in_specs=[SMEM],
        out_specs=SMEM,
        cost_estimate=pl.CostEstimate(flops=30000000000, bytes_accessed=64, transcendentals=0),
    )(place)
    near, table = lax.optimization_barrier((lax.all_to_all(acts, RING, 0, 0, tiled=True), table))

    (parts,) = call(
        sums_kernel, [jax.ShapeDtypeStruct((8, 3, 32, 896), BF16)],
        (table, near, exchange(near, "core"), *weights), [pltpu.VMEM((2, 256, 1024), BF16)],
        6 * 256 * 1024 * 896, 8000000,
    )
    parts = lax.all_to_all(parts, "y", 0, 0, tiled=True)
    gate_value, hidden_grad, up_value = (jnp.sum(parts[:, k].astype(F32), axis=0) for k in range(3))
    sig = jax.nn.sigmoid(gate_value)
    silu = gate_value * sig
    hidden = (silu * up_value).astype(BF16)
    gate_grad = (hidden_grad * up_value * sig * (1.0 + gate_value * (1.0 - sig))).astype(BF16)
    up_grad = (hidden_grad * silu).astype(BF16)
    rows = jnp.stack([hidden, gate_grad, up_grad])
    rows = lax.all_to_all(jnp.broadcast_to(rows[None], (8, 3, 32, 896)), "y", 0, 0, tiled=True)
    terms = jax.ShapeDtypeStruct((8, 2, 128, 128), F32)
    mine, theirs = call(
        output_kernel, [terms, terms], (table, rows, *weights), [pltpu.VMEM((2, 8, 2, 128, 128), F32)],
        6 * 256 * 1024 * 896, 8000000,
    )
    terms = (mine + exchange(theirs, "core")).astype(BF16)
    terms = lax.all_to_all(terms, RING, 0, 0, tiled=True)
    both = jnp.sum(terms.astype(F32), axis=0).astype(BF16)
    return both[0], both[1]


def solution(mesh):
    fine = Mesh(mesh.devices.reshape(SIZES), AXES)
    acts = P(("zh", "x"), ("y", "zl", "core"))
    weights = P(("y", "zh", "x"), ("zl", "core"))
    return jax.shard_map(
        on_device,
        mesh=fine,
        in_specs=(acts, weights, weights, weights, acts),
        out_specs=(acts, acts),
        check_vma=False,
    )
```

```python
import jax
import jax.numpy as jnp
from jax import lax
from jax.experimental import pallas as pl
from jax.experimental.pallas import tpu as pltpu
from jax.sharding import Mesh, PartitionSpec as P

AXES = ("y", "zl", "core", "zh", "x")
SIZES = (8, 4, 2, 2, 4)
RING = ("zh", "zl")
NT = (((1,), (1,)), ((), ()))
F32, BF16 = jnp.float32, jnp.bfloat16
STEPS = (0, 3, 1, 2)
GATE, DOWN, UP = 0, 1, 2
WHICH = (0, 1, 0)
SMEM = pl.BlockSpec(memory_space=pltpu.SMEM)
VMEM = pl.BlockSpec(memory_space=pltpu.VMEM)


def call(kernel, outs, operands, scratch, flops, moved):
    return pl.pallas_call(
        kernel,
        out_shape=outs,
        in_specs=[SMEM] + [VMEM] * (len(operands) - 1),
        out_specs=[VMEM] * len(outs),
        scratch_shapes=scratch,
        cost_estimate=pl.CostEstimate(flops=flops, bytes_accessed=moved, transcendentals=0),
        compiler_params=pltpu.CompilerParams(vmem_limit_bytes=12 << 20),
    )(*operands)


def shift(values, step):
    return lax.ppermute(values, "x", [(i, (i + step) % 4) for i in range(4)])


def exchange(values, axis):
    return lax.ppermute(values, axis, [(0, 1), (1, 0)])


def split_kernel(place, gate, down, up, keep, send):
    low = place[1] == 0
    for k, weight in enumerate((gate, down, up)):
        left, right = weight[:, :896], weight[:, 896:]
        rows = pl.ds(128 * k, 128)
        keep[rows] = jnp.where(low, left, right)
        send[rows] = jnp.where(low, right, left)


def table_kernel(place, out):
    for other_zh in (0, 1):
        for slot in range(4):
            zh = 1 - place[1] if other_zh else place[1]
            out[4 * other_zh + slot] = 4 * zh + (place[0] + STEPS[slot]) % 4
    out[8] = place[2]


def pack_kernel(place, b0, b1, b2, b3, out):
    for slot, block in enumerate((b0, b1, b2, b3)):
        for k in range(3):
            out[k, 128 * slot : 128 * slot + 128] = block[128 * k : 128 * k + 128]


def hold_kernel(place, block, out):
    out[...] = block[...]


def spread_kernel(place, tokens, grad, out):
    for i in range(8):
        out[i, 0] = tokens[...]
        out[i, 1] = grad[...]


def sums_kernel(table, near, other, kept, moved, out, wide):
    for other_zh in (0, 1):
        for slot in range(4):
            f = table[4 * other_zh + slot]
            same = f % 2 == table[8]
            for t in (0, 1):
                for which in (0, 1):
                    tile = jnp.where(same, near[4 * t + f // 2, which], other[4 * t + f // 2, which])
                    wide[which, pl.ds(128 * t, 128), pl.ds(512 * other_zh + 128 * slot, 128)] = tile
    for k in range(3):
        total = jnp.dot(wide[WHICH[k], :, :512], kept[k], preferred_element_type=F32)
        total = total + jnp.dot(wide[WHICH[k], :, 512:], moved[k], preferred_element_type=F32)
        out[:, k] = total.astype(BF16).reshape(8, 32, 896)


def output_kernel(table, acts, kept, moved, mine, theirs):
    hidden, gate_grad, up_grad = (acts[:, k].reshape(256, 896) for k in range(3))

    def product(rows, block):
        return lax.dot_general(rows, block, NT, preferred_element_type=F32)

    for other_zh, rows in enumerate((kept, moved)):
        mixed = product(hidden, rows[DOWN])
        grad = product(gate_grad, rows[GATE]) + product(up_grad, rows[UP])
        for odd in (0, 1):

            @pl.when((table[0] + table[8]) % 2 == odd)
            def _(other_zh=other_zh, mixed=mixed, grad=grad, odd=odd):
                for slot in range(4):
                    f = table[4 * other_zh + slot]
                    out = theirs if (odd + STEPS[slot]) % 2 else mine
                    for t in (0, 1):
                        part = (slice(128 * t, 128 * t + 128), slice(128 * slot, 128 * slot + 128))
                        out[4 * t + f // 2, 0] = mixed[part]
                        out[4 * t + f // 2, 1] = grad[part]


def final_kernel(table, terms, mixed, tokens_grad):
    for k, out in enumerate((mixed, tokens_grad)):
        total = terms[0, k].astype(F32)
        for i in range(1, 8):
            total = total + terms[i, k].astype(F32)
        out[...] = total.astype(BF16)


def on_device(tokens, gate_weight, up_weight, down_weight, grad_mixed):
    place = jnp.stack([lax.axis_index("x"), lax.axis_index("zh"), lax.axis_index("core")])
    half = jax.ShapeDtypeStruct((384, 896), BF16)
    keep, send = call(split_kernel, [half, half], (place, gate_weight, down_weight, up_weight), [], 0, 3000000)
    block = exchange(send, "zh")
    kept = (shift(keep, 1), shift(keep, -1), shift(keep, 2))
    packed = jax.ShapeDtypeStruct((3, 512, 896), BF16)
    (first,) = call(pack_kernel, [packed], (place, keep, *kept), [], 0, 0)
    (hold,) = call(hold_kernel, [half], (place, block), [], 30000000000, 1400000)
    block, first, tokens = lax.optimization_barrier((hold, first, tokens))
    moved = (block, shift(block, 1), shift(block, -1), shift(block, 2))
    (second,) = call(pack_kernel, [packed], (place, *moved), [], 0, 0)
    weights = (first, second)
    (acts,) = call(
        spread_kernel, [jax.ShapeDtypeStruct((8, 2, 128, 128), BF16)], (place, tokens, grad_mixed), [], 30000000000, 1000000
    )
    table = pl.pallas_call(
        table_kernel,
        out_shape=jax.ShapeDtypeStruct((9,), jnp.int32),
        in_specs=[SMEM],
        out_specs=SMEM,
        cost_estimate=pl.CostEstimate(flops=30000000000, bytes_accessed=64, transcendentals=0),
    )(place)
    near, table = lax.optimization_barrier((lax.all_to_all(acts, RING, 0, 0, tiled=True), table))

    (parts,) = call(
        sums_kernel, [jax.ShapeDtypeStruct((8, 3, 32, 896), BF16)],
        (table, near, exchange(near, "core"), *weights), [pltpu.VMEM((2, 256, 1024), BF16)],
        6 * 256 * 1024 * 896, 8000000,
    )
    parts = lax.all_to_all(parts, "y", 0, 0, tiled=True)
    gate_value, hidden_grad, up_value = (jnp.sum(parts[:, k].astype(F32), axis=0) for k in range(3))
    sig = jax.nn.sigmoid(gate_value)
    silu = gate_value * sig
    hidden = (silu * up_value).astype(BF16)
    gate_grad = (hidden_grad * up_value * sig * (1.0 + gate_value * (1.0 - sig))).astype(BF16)
    up_grad = (hidden_grad * silu).astype(BF16)
    rows = jnp.stack([hidden, gate_grad, up_grad])
    rows = lax.all_to_all(jnp.broadcast_to(rows[None], (8, 3, 32, 896)), "y", 0, 0, tiled=True)
    terms = jax.ShapeDtypeStruct((8, 2, 128, 128), F32)
    mine, theirs = call(
        output_kernel, [terms, terms], (table, rows, *weights), [],
        6 * 256 * 1024 * 896, 8000000,
    )
    terms = (mine + exchange(theirs, "core")).astype(BF16)
    terms = lax.all_to_all(terms, RING, 0, 0, tiled=True)
    out = jax.ShapeDtypeStruct((128, 128), BF16)
    return tuple(call(final_kernel, [out, out], (table, terms), [], 0, 0))


def solution(mesh):
    fine = Mesh(mesh.devices.reshape(SIZES), AXES)
    acts = P(("zh", "x"), ("y", "zl", "core"))
    weights = P(("y", "zh", "x"), ("zl", "core"))
    return jax.shard_map(
        on_device,
        mesh=fine,
        in_specs=(acts, weights, weights, weights, acts),
        out_specs=(acts, acts),
        check_vma=False,
    )
```

```python
import jax
import jax.numpy as jnp
from jax import lax
from jax.experimental import pallas as pl
from jax.experimental.pallas import tpu as pltpu
from jax.sharding import Mesh, PartitionSpec as P

AXES = ("y", "zl", "core", "zh", "x")
SIZES = (8, 4, 2, 2, 4)
RING = ("zh", "zl")
NT = (((1,), (1,)), ((), ()))
F32, BF16 = jnp.float32, jnp.bfloat16
STEPS = (0, 3, 1, 2)
GATE, DOWN, UP = 0, 1, 2
WHICH = (0, 1, 0)
SMEM = pl.BlockSpec(memory_space=pltpu.SMEM)
VMEM = pl.BlockSpec(memory_space=pltpu.VMEM)


def call(kernel, outs, operands, scratch, flops, moved):
    return pl.pallas_call(
        kernel,
        out_shape=outs,
        in_specs=[SMEM] + [VMEM] * (len(operands) - 1),
        out_specs=[VMEM] * len(outs),
        scratch_shapes=scratch,
        cost_estimate=pl.CostEstimate(flops=flops, bytes_accessed=moved, transcendentals=0),
        compiler_params=pltpu.CompilerParams(vmem_limit_bytes=12 << 20),
    )(*operands)


def shift(values, step):
    return lax.ppermute(values, "x", [(i, (i + step) % 4) for i in range(4)])


def exchange(values, axis):
    return lax.ppermute(values, axis, [(0, 1), (1, 0)])


def split_kernel(place, gate, down, up, keep, send):
    low = place[1] == 0
    for k, weight in enumerate((gate, down, up)):
        left, right = weight[:, :896], weight[:, 896:]
        rows = pl.ds(128 * k, 128)
        keep[rows] = jnp.where(low, left, right)
        send[rows] = jnp.where(low, right, left)


def table_kernel(place, out):
    for other_zh in (0, 1):
        for slot in range(4):
            zh = 1 - place[1] if other_zh else place[1]
            out[4 * other_zh + slot] = 4 * zh + (place[0] + STEPS[slot]) % 4
    out[8] = place[2]


def pack_kernel(place, b0, b1, b2, b3, out):
    for slot, block in enumerate((b0, b1, b2, b3)):
        for k in range(3):
            out[k, 128 * slot : 128 * slot + 128] = block[128 * k : 128 * k + 128]


def hold_kernel(place, block, out):
    out[...] = block[...]


def spread_kernel(place, tokens, grad, out):
    for i in range(8):
        out[i, 0] = tokens[...]
        out[i, 1] = grad[...]


def sums_kernel(table, near, other, kept, b0, b1, b2, b3, out, moved, wide, sems):
    copies = [
        [
            pltpu.make_async_copy(
                block.at[pl.ds(128 * k, 128)], moved.at[k, pl.ds(128 * slot, 128)], sems.at[4 * k + slot]
            )
            for slot, block in enumerate((b0, b1, b2, b3))
        ]
        for k in range(3)
    ]
    for k in range(3):
        for copy in copies[k]:
            copy.start()
    for other_zh in (0, 1):
        for slot in range(4):
            f = table[4 * other_zh + slot]
            same = f % 2 == table[8]
            for t in (0, 1):
                for which in (0, 1):
                    tile = jnp.where(same, near[4 * t + f // 2, which], other[4 * t + f // 2, which])
                    wide[which, pl.ds(128 * t, 128), pl.ds(512 * other_zh + 128 * slot, 128)] = tile
    for k in range(3):
        total = jnp.dot(wide[WHICH[k], :, :512], kept[k], preferred_element_type=F32)
        for copy in copies[k]:
            copy.wait()
        total = total + jnp.dot(wide[WHICH[k], :, 512:], moved[k], preferred_element_type=F32)
        out[:, k] = total.astype(BF16).reshape(8, 32, 896)


def output_kernel(table, acts, kept, moved, mine, theirs, held):
    hidden, gate_grad, up_grad = (acts[:, k].reshape(256, 896) for k in range(3))

    def product(rows, block):
        return lax.dot_general(rows, block, NT, preferred_element_type=F32)

    for other_zh, rows in enumerate((kept, moved)):
        mixed = product(hidden, rows[DOWN])
        grad = product(gate_grad, rows[GATE]) + product(up_grad, rows[UP])
        for slot in range(4):
            f = table[4 * other_zh + slot]
            side = (f + table[8]) % 2
            for t in (0, 1):
                part = (slice(128 * t, 128 * t + 128), slice(128 * slot, 128 * slot + 128))
                held[side, 4 * t + f // 2, 0] = mixed[part]
                held[side, 4 * t + f // 2, 1] = grad[part]
    mine[...] = held[0]
    theirs[...] = held[1]


def on_device(tokens, gate_weight, up_weight, down_weight, grad_mixed):
    place = jnp.stack([lax.axis_index("x"), lax.axis_index("zh"), lax.axis_index("core")])
    half = jax.ShapeDtypeStruct((384, 896), BF16)
    keep, send = call(split_kernel, [half, half], (place, gate_weight, down_weight, up_weight), [], 0, 3000000)
    block = exchange(send, "zh")
    kept = (shift(keep, 1), shift(keep, -1), shift(keep, 2))
    packed = jax.ShapeDtypeStruct((3, 512, 896), BF16)
    (first,) = call(pack_kernel, [packed], (place, keep, *kept), [], 0, 0)
    (hold,) = call(hold_kernel, [half], (place, block), [], 30000000000, 1400000)
    block, first, tokens = lax.optimization_barrier((hold, first, tokens))
    moved = (block, shift(block, 1), shift(block, -1), shift(block, 2))
    (acts,) = call(
        spread_kernel, [jax.ShapeDtypeStruct((8, 2, 128, 128), BF16)], (place, tokens, grad_mixed), [], 30000000000, 1000000
    )
    table = pl.pallas_call(
        table_kernel,
        out_shape=jax.ShapeDtypeStruct((9,), jnp.int32),
        in_specs=[SMEM],
        out_specs=SMEM,
        cost_estimate=pl.CostEstimate(flops=30000000000, bytes_accessed=64, transcendentals=0),
    )(place)
    near, table = lax.optimization_barrier((lax.all_to_all(acts, RING, 0, 0, tiled=True), table))

    parts, second = pl.pallas_call(
        sums_kernel,
        out_shape=[jax.ShapeDtypeStruct((8, 3, 32, 896), BF16), packed],
        in_specs=[SMEM] + [VMEM] * 3 + [pl.BlockSpec(memory_space=pl.ANY)] * 4,
        out_specs=[VMEM, VMEM],
        scratch_shapes=[pltpu.VMEM((2, 256, 1024), BF16), pltpu.SemaphoreType.DMA((12,))],
        cost_estimate=pl.CostEstimate(flops=6 * 256 * 1024 * 896, bytes_accessed=8000000, transcendentals=0),
        compiler_params=pltpu.CompilerParams(vmem_limit_bytes=12 << 20),
    )(table, near, exchange(near, "core"), first, *moved)
    parts = lax.all_to_all(parts, "y", 0, 0, tiled=True)
    gate_value, hidden_grad, up_value = (jnp.sum(parts[:, k].astype(F32), axis=0) for k in range(3))
    sig = jax.nn.sigmoid(gate_value)
    silu = gate_value * sig
    hidden = (silu * up_value).astype(BF16)
    gate_grad = (hidden_grad * up_value * sig * (1.0 + gate_value * (1.0 - sig))).astype(BF16)
    up_grad = (hidden_grad * silu).astype(BF16)
    rows = jnp.stack([hidden, gate_grad, up_grad])
    rows = lax.all_to_all(jnp.broadcast_to(rows[None], (8, 3, 32, 896)), "y", 0, 0, tiled=True)
    terms = jax.ShapeDtypeStruct((8, 2, 128, 128), F32)
    mine, theirs = call(
        output_kernel, [terms, terms], (table, rows, first, second), [pltpu.VMEM((2, 8, 2, 128, 128), F32)],
        6 * 256 * 1024 * 896, 8000000,
    )
    terms = (mine + exchange(theirs, "core")).astype(BF16)
    terms = lax.all_to_all(terms, RING, 0, 0, tiled=True)
    both = jnp.sum(terms.astype(F32), axis=0).astype(BF16)
    return both[0], both[1]


def solution(mesh):
    fine = Mesh(mesh.devices.reshape(SIZES), AXES)
    acts = P(("zh", "x"), ("y", "zl", "core"))
    weights = P(("y", "zh", "x"), ("zl", "core"))
    return jax.shard_map(
        on_device,
        mesh=fine,
        in_specs=(acts, weights, weights, weights, acts),
        out_specs=(acts, acts),
        check_vma=False,
    )
```

```python
import jax
import jax.numpy as jnp
from jax import lax
from jax.experimental import pallas as pl
from jax.experimental.pallas import tpu as pltpu
from jax.sharding import Mesh, PartitionSpec as P

AXES = ("y", "zl", "core", "zh", "x")
SIZES = (8, 4, 2, 2, 4)
RING = ("zh", "zl")
NT = (((1,), (1,)), ((), ()))
F32, BF16 = jnp.float32, jnp.bfloat16
STEPS = (0, 3, 1, 2)
GATE, DOWN, UP = 0, 1, 2
WHICH = (0, 1, 0)
SMEM = pl.BlockSpec(memory_space=pltpu.SMEM)
VMEM = pl.BlockSpec(memory_space=pltpu.VMEM)


def call(kernel, outs, operands, scratch, flops, moved):
    return pl.pallas_call(
        kernel,
        out_shape=outs,
        in_specs=[SMEM] + [VMEM] * (len(operands) - 1),
        out_specs=[VMEM] * len(outs),
        scratch_shapes=scratch,
        cost_estimate=pl.CostEstimate(flops=flops, bytes_accessed=moved, transcendentals=0),
        compiler_params=pltpu.CompilerParams(vmem_limit_bytes=24 << 20),
    )(*operands)


def shift(values, step):
    return lax.ppermute(values, "x", [(i, (i + step) % 4) for i in range(4)])


def exchange(values, axis):
    return lax.ppermute(values, axis, [(0, 1), (1, 0)])


def split_kernel(place, gate, down, up, keep, send):
    low = place[1] == 0
    for k, weight in enumerate((gate, down, up)):
        left, right = weight[:, :896], weight[:, 896:]
        rows = pl.ds(128 * k, 128)
        keep[rows] = jnp.where(low, left, right)
        send[rows] = jnp.where(low, right, left)


def table_kernel(place, out):
    for other_zh in (0, 1):
        for slot in range(4):
            zh = 1 - place[1] if other_zh else place[1]
            out[4 * other_zh + slot] = 4 * zh + (place[0] + STEPS[slot]) % 4
    out[8] = place[2]


def pack_kernel(place, b0, b1, b2, b3, out):
    for slot, block in enumerate((b0, b1, b2, b3)):
        for k in range(3):
            out[k, 128 * slot : 128 * slot + 128] = block[128 * k : 128 * k + 128]


def hold_kernel(place, block, out):
    out[...] = block[...]


def spread_kernel(place, tokens, grad, out):
    for i in range(8):
        out[i, 0] = tokens[...]
        out[i, 1] = grad[...]


def sums_kernel(table, near, other, kept, moved, out, wide):
    for other_zh in (0, 1):
        for slot in range(4):
            f = table[4 * other_zh + slot]
            same = f % 2 == table[8]
            for t in (0, 1):
                for which in (0, 1):
                    tile = jnp.where(same, near[4 * t + f // 2, which], other[4 * t + f // 2, which])
                    wide[which, pl.ds(128 * t, 128), pl.ds(512 * other_zh + 128 * slot, 128)] = tile
    for k in range(3):
        total = jnp.dot(wide[WHICH[k], :, :512], kept[k], preferred_element_type=F32)
        total = total + jnp.dot(wide[WHICH[k], :, 512:], moved[k], preferred_element_type=F32)
        out[:, k] = total.astype(BF16).reshape(8, 32, 896)


def output_kernel(table, acts, kept, moved, mine, theirs, held):
    hidden, gate_grad, up_grad = (acts[:, k].reshape(256, 896) for k in range(3))

    def product(rows, block):
        return lax.dot_general(rows, block, NT, preferred_element_type=F32)

    for other_zh, rows in enumerate((kept, moved)):
        mixed = product(hidden, rows[DOWN])
        grad = product(gate_grad, rows[GATE]) + product(up_grad, rows[UP])
        for slot in range(4):
            f = table[4 * other_zh + slot]
            side = (f + table[8]) % 2
            for t in (0, 1):
                part = (slice(128 * t, 128 * t + 128), slice(128 * slot, 128 * slot + 128))
                held[side, 4 * t + f // 2, 0] = mixed[part]
                held[side, 4 * t + f // 2, 1] = grad[part]
    mine[...] = held[0]
    theirs[...] = held[1]


def on_device(tokens, gate_weight, up_weight, down_weight, grad_mixed):
    place = jnp.stack([lax.axis_index("x"), lax.axis_index("zh"), lax.axis_index("core")])
    half = jax.ShapeDtypeStruct((384, 896), BF16)
    keep, send = call(split_kernel, [half, half], (place, gate_weight, down_weight, up_weight), [], 0, 3000000)
    block = exchange(send, "zh")
    kept = (shift(keep, 1), shift(keep, -1), shift(keep, 2))
    packed = jax.ShapeDtypeStruct((3, 512, 896), BF16)
    (first,) = call(pack_kernel, [packed], (place, keep, *kept), [], 0, 0)
    (hold,) = call(hold_kernel, [half], (place, block), [], 30000000000, 1400000)
    block, first, tokens = lax.optimization_barrier((hold, first, tokens))
    moved = (block, shift(block, 1), shift(block, -1), shift(block, 2))
    (second,) = call(pack_kernel, [packed], (place, *moved), [], 0, 0)
    weights = (first, second)
    (acts,) = call(
        spread_kernel, [jax.ShapeDtypeStruct((8, 2, 128, 128), BF16)], (place, tokens, grad_mixed), [], 30000000000, 1000000
    )
    table = pl.pallas_call(
        table_kernel,
        out_shape=jax.ShapeDtypeStruct((9,), jnp.int32),
        in_specs=[SMEM],
        out_specs=SMEM,
        cost_estimate=pl.CostEstimate(flops=30000000000, bytes_accessed=64, transcendentals=0),
    )(place)
    near, table = lax.optimization_barrier((lax.all_to_all(acts, RING, 0, 0, tiled=True), table))

    (parts,) = call(
        sums_kernel, [jax.ShapeDtypeStruct((8, 3, 32, 896), BF16)],
        (table, near, exchange(near, "core"), *weights), [pltpu.VMEM((2, 256, 1024), BF16)],
        6 * 256 * 1024 * 896, 8000000,
    )
    parts = lax.all_to_all(parts, "y", 0, 0, tiled=True)
    gate_value, hidden_grad, up_value = (jnp.sum(parts[:, k].astype(F32), axis=0) for k in range(3))
    sig = jax.nn.sigmoid(gate_value)
    silu = gate_value * sig
    hidden = (silu * up_value).astype(BF16)
    gate_grad = (hidden_grad * up_value * sig * (1.0 + gate_value * (1.0 - sig))).astype(BF16)
    up_grad = (hidden_grad * silu).astype(BF16)
    rows = jnp.stack([hidden, gate_grad, up_grad])
    rows = lax.all_to_all(jnp.broadcast_to(rows[None], (8, 3, 32, 896)), "y", 0, 0, tiled=True)
    terms = jax.ShapeDtypeStruct((8, 2, 128, 128), F32)
    mine, theirs = call(
        output_kernel, [terms, terms], (table, rows, *weights), [pltpu.VMEM((2, 8, 2, 128, 128), F32)],
        6 * 256 * 1024 * 896, 8000000,
    )
    terms = (mine + exchange(theirs, "core")).astype(BF16)
    terms = lax.all_to_all(terms, RING, 0, 0, tiled=True)
    both = jnp.sum(terms.astype(F32), axis=0).astype(BF16)
    return both[0], both[1]


def solution(mesh):
    fine = Mesh(mesh.devices.reshape(SIZES), AXES)
    acts = P(("zh", "x"), ("y", "zl", "core"))
    weights = P(("y", "zh", "x"), ("zl", "core"))
    return jax.shard_map(
        on_device,
        mesh=fine,
        in_specs=(acts, weights, weights, weights, acts),
        out_specs=(acts, acts),
        check_vma=False,
    )
```
